32 devices in a mesh: fsdp: 8 (over z, core), tp: 4 (over y, x).
Axes of the slice: x: 2, y: 2, z: 4, core: 2. Of those that a mesh axis runs over, the one named last changes fastest.
Arguments:
- master_qo: float32 [2, 5120, 8192], P(None, ('fsdp', 'tp')), may hold values from -0.078125 to 0.078125
- master_kv: float32 [2, 5120, 1024], P(None, ('fsdp', 'tp')), may hold values from -0.078125 to 0.078125
- moment1_qo: float32 [2, 5120, 8192], P(None, ('fsdp', 'tp')), may hold values from -0.00061035156 to 0.00061035156
- moment1_kv: float32 [2, 5120, 1024], P(None, ('fsdp', 'tp')), may hold values from -0.00061035156 to 0.00061035156
- moment2_qo: float32 [2, 5120, 8192], P(None, ('fsdp', 'tp')), may hold values from 0 to 1, as said below
- moment2_kv: float32 [2, 5120, 1024], P(None, ('fsdp', 'tp')), may hold values from 0 to 1, as said below
- grad_qo: float32 [2, 5120, 8192], P(None, ('fsdp', 'tp')), may hold values from -13 to 13
- grad_kv: float32 [2, 5120, 1024], P(None, ('fsdp', 'tp')), may hold values from -13 to 13
- hidden: bfloat16 [512, 5120], P(('fsdp', 'tp')), may hold values from -3 to 3
- norm_gain: float32 [5120], replicated, may hold values from 0.5 to 1.5
- qk_gain: float32 [2, 128], replicated, may hold values from 0.25 to 1.75
- key_cache: bfloat16 [512, 8, 128, 128], P('fsdp', 'tp'), may hold values from -310 to 310
- cached_value_rows: bfloat16 [512, 8, 128, 128], P('fsdp', 'tp'), may hold values from -18 to 18
- lengths: int32 [512], P('fsdp'), may hold values from 1 to 128, as said below
Outputs:
- new_master_qo: float32 [2, 5120, 8192], P(None, ('fsdp', 'tp'))
- new_master_kv: float32 [2, 5120, 1024], P(None, ('fsdp', 'tp'))
- new_moment1_qo: float32 [2, 5120, 8192], P(None, ('fsdp', 'tp'))
- new_moment1_kv: float32 [2, 5120, 1024], P(None, ('fsdp', 'tp'))
- new_moment2_qo: float32 [2, 5120, 8192], P(None, ('fsdp', 'tp'))
- new_moment2_kv: float32 [2, 5120, 1024], P(None, ('fsdp', 'tp'))
- new_hidden: bfloat16 [512, 5120], P(('fsdp', 'tp'))
- new_key: bfloat16 [512, 8, 128], P('fsdp', 'tp')
- new_value: bfloat16 [512, 8, 128], P('fsdp', 'tp')
The draws below stay inside these ranges and needn't reach their ends.
Inputs may be any that keep to these rules, and one draw needn't show every extreme that they name: `moment2_qo`: positive. `moment2_kv`: positive. `lengths`: some row holds 128 in every draw.
All inputs are finite; a program needn't handle non-finite values.
Results may differ from the reference program's by a relative error of at most 0.012.
The reference program's roundings to bfloat16 on the way count: a program that leaves them out, or rounds other values in their place, can miss the bound.
Values may be sent and summed in bfloat16 or wider, within the bound.
No kernel may reach another device: no remote copies, remote signals or barrier semaphores. Data moves between devices by JAX's collectives and lax.ppermute only.
A program may use at most 320 MiB of HBM per device.

```python
import math
import jax
import jax.numpy as jnp
from jax import lax

MODEL_WIDTH = 5120
QUERY_HEADS = 64
KEY_VALUE_HEADS = 8
HEAD_SIZE = 128
CACHE_SLOTS = 128
QW = 8192
KW = 1024
BATCH_ROWS_ALL = 512
NTOT = 94371840


def grad_scales(key, tensor_shape, ramp_top):
    random_subkeys = jax.random.split(key, 2)
    row_total = tensor_shape[1]
    ramp_curve = ramp_top ** (0.5 * jnp.arange(row_total, dtype=jnp.float32) / row_total)
    row_scale = jnp.exp(jax.random.uniform(random_subkeys[0], (tensor_shape[0], row_total, 1), minval=0.0, maxval=math.log(10.0)))
    col_scale = jnp.exp(jax.random.uniform(random_subkeys[1], (tensor_shape[0], 1, tensor_shape[2]), minval=0.0, maxval=math.log(10.0)))
    return 0.01 * ramp_curve[None, :, None] * row_scale * col_scale


def draw_grad_qo(key, part):
    key = jax.random.fold_in(key, 11)
    random_subkeys = jax.random.split(key, 2)
    tensor_shape = (2, MODEL_WIDTH, QUERY_HEADS * HEAD_SIZE)
    base_draw = jnp.clip(jax.random.normal(random_subkeys[1], tensor_shape), -6.0, 6.0)
    return (grad_scales(random_subkeys[0], tensor_shape, 3.0) * base_draw).astype(jnp.float32)


def draw_grad_kv(key, part):
    key = jax.random.fold_in(key, 12)
    random_subkeys = jax.random.split(key, 2)
    tensor_shape = (2, MODEL_WIDTH, KEY_VALUE_HEADS * HEAD_SIZE)
    base_draw = jnp.clip(jax.random.normal(random_subkeys[1], tensor_shape), -6.0, 6.0)
    return (grad_scales(random_subkeys[0], tensor_shape, 3.0) * base_draw).astype(jnp.float32)


def moment_entry_name(key, tensor_shape, exponent):
    parameter_count = 2 * MODEL_WIDTH * QUERY_HEADS * HEAD_SIZE + 2 * MODEL_WIDTH * KEY_VALUE_HEADS * HEAD_SIZE
    unit = jax.random.uniform(key, tensor_shape, minval=0.0, maxval=1.0)
    lower = 0.25 / parameter_count
    upper = 16.0 / parameter_count
    return lower * (upper / lower) ** unit ** exponent


def draw_moment2_qo(key, part):
    key = jax.random.fold_in(key, 17)
    return moment_entry_name(key, (2, MODEL_WIDTH, QUERY_HEADS * HEAD_SIZE), 1.0).astype(jnp.float32)


def draw_moment2_kv(key, part):
    key = jax.random.fold_in(key, 18)
    return moment_entry_name(key, (2, MODEL_WIDTH, KEY_VALUE_HEADS * HEAD_SIZE), 1.0).astype(jnp.float32)


def draw_key_cache(key, part):
    key = jax.random.fold_in(key, 23)
    random_subkeys = jax.random.split(key, 1)
    tensor_shape = (BATCH_ROWS_ALL, KEY_VALUE_HEADS, CACHE_SLOTS, HEAD_SIZE)
    base_draw = jnp.clip(jax.random.normal(random_subkeys[0], tensor_shape), -6.0, 6.0)
    return base_draw.astype(jnp.bfloat16)


def draw_lengths(key, part):
    key = jax.random.fold_in(key, 31)
    random_subkeys = jax.random.split(key, 2)
    drawn_len = jax.random.randint(random_subkeys[0], (BATCH_ROWS_ALL,), 1, CACHE_SLOTS + 1)
    fullest = jax.random.randint(random_subkeys[1], (), 0, BATCH_ROWS_ALL)
    return jnp.where(jnp.arange(BATCH_ROWS_ALL, dtype=jnp.int32) == fullest, CACHE_SLOTS, drawn_len).astype(jnp.int32)


def level_of(rng, shape, pieces, least, top_value):
    factor_of = 1.0
    for position, parts in pieces:
        heights = jax.random.uniform(jax.random.fold_in(jax.random.fold_in(rng, 6), position), (parts,), jnp.float32, least / len(pieces), top_value / len(pieces))
        factor_of = factor_of * jnp.repeat(jnp.exp(heights), shape[position] // parts).reshape((-1,) + (1,) * (len(shape) - 1 - position))
    return factor_of


def noise(key, dims, scale, bound, cuts=(), kind=jnp.bfloat16):
    entries = jax.random.normal(key, dims, jnp.float32) * scale
    if len(cuts) > 0:
        entries = level_of(key, dims, cuts, -0.22, 0.18) * entries
    return jnp.clip(entries, min=-bound, max=bound).astype(kind)


def setup_inputs(seed: int = 0) -> dict:
    splits = jax.random.split(jax.random.key(seed), 15)
    return {
        "master_qo": noise(splits[0], (2, MODEL_WIDTH, QW), MODEL_WIDTH ** -0.5, 0.078125, ((1, 32),), jnp.float32),
        "master_kv": noise(splits[1], (2, MODEL_WIDTH, KW), MODEL_WIDTH ** -0.5, 0.078125, ((1, 32),), jnp.float32),
        "moment1_qo": noise(splits[2], (2, MODEL_WIDTH, QW), NTOT ** -0.5, 0.00061035156, ((1, 32),), jnp.float32),
        "moment1_kv": noise(splits[3], (2, MODEL_WIDTH, KW), NTOT ** -0.5, 0.00061035156, ((1, 32),), jnp.float32),
        "moment2_qo": draw_moment2_qo(jax.random.fold_in(splits[14], 71), 0),
        "moment2_kv": draw_moment2_kv(jax.random.fold_in(splits[14], 71), 0),
        "grad_qo": draw_grad_qo(jax.random.fold_in(splits[14], 71), 0),
        "grad_kv": draw_grad_kv(jax.random.fold_in(splits[14], 71), 0),
        "hidden": noise(splits[8], (BATCH_ROWS_ALL, MODEL_WIDTH), 0.5, 3.0, ((0, 32),)),
        "norm_gain": jnp.clip(1.0 + 0.1 * jax.random.normal(splits[9], (MODEL_WIDTH,), jnp.float32), 0.5, 1.5),
        "qk_gain": jnp.clip(1.0 + 0.15 * jax.random.normal(splits[10], (2, HEAD_SIZE), jnp.float32), 0.25, 1.75),
        "key_cache": draw_key_cache(jax.random.fold_in(splits[14], 71), 0),
        "cached_value_rows": noise(splits[12], (BATCH_ROWS_ALL, KEY_VALUE_HEADS, CACHE_SLOTS, HEAD_SIZE), 3.0, 18.0, ((0, 8), (1, 4))),
        "lengths": draw_lengths(jax.random.fold_in(splits[14], 71), 0),
    }


clip_limit = 1.0
beta_one = 0.9
beta_two = 0.95
learn_rate = 0.01
decay_rate = 0.1
adam_step = 10.0
eps_adam = 1e-08
eps_norm = 1e-06
rope_base = 1000000.0

def adam_update(master, moment_one, moment_two, gradient, clip_factor):
    clipped = gradient * clip_factor
    moment_one = beta_one * moment_one + (1.0 - beta_one) * clipped
    moment_two = beta_two * moment_two + (1.0 - beta_two) * clipped * clipped
    fix_one = 1.0 - beta_one ** adam_step
    fix_two = 1.0 - beta_two ** adam_step
    step_size = moment_one / fix_one / (jnp.sqrt(moment_two / fix_two) + eps_adam)
    master = master - learn_rate * (step_size + decay_rate * master)
    return (master, moment_one, moment_two)

def root_scale(values, gain_vec):
    mean_square = lax.optimization_barrier(jnp.mean(values * values, axis=-1, keepdims=True))
    return values * lax.rsqrt(mean_square + eps_norm) * gain_vec

def rotate(values, positions):
    half_dim = values.shape[-1] // 2
    frequency = rope_base ** (-(jnp.arange(half_dim, dtype=jnp.float32) * 2.0) / values.shape[-1])
    angles = positions.astype(jnp.float32)[:, None] * frequency[None, :]
    cosine = jnp.cos(angles)[:, None, :]
    sine_part = jnp.sin(angles)[:, None, :]
    first_half = values[..., :half_dim]
    second = values[..., half_dim:]
    return jnp.concatenate([first_half * cosine - second * sine_part, second * cosine + first_half * sine_part], axis=-1)

def attend(queries, key_new, value_new, qk_gain, key_cache, cached_value_rows, lengths):
    row_count = queries.shape[0]
    kv_heads = key_cache.shape[1]
    head_dim = key_cache.shape[-1]
    queries = queries.reshape(row_count, -1, head_dim)
    key_new = key_new.reshape(row_count, kv_heads, head_dim)
    rotated = rotate(root_scale(queries, qk_gain[0]), lengths).astype(jnp.bfloat16)
    new_key = rotate(root_scale(key_new, qk_gain[1]), lengths).astype(jnp.bfloat16)
    new_value = value_new.reshape(row_count, kv_heads, head_dim).astype(jnp.bfloat16)
    group_size = rotated.shape[1] // kv_heads
    grouped = rotated.reshape(row_count, kv_heads, group_size, head_dim).astype(jnp.float32)
    inv_root = 1.0 / math.sqrt(head_dim)
    scores = jnp.einsum('bkgd,bkcd->bkgc', grouped, key_cache.astype(jnp.float32)) * inv_root
    self_score = lax.optimization_barrier(jnp.sum(grouped * new_key.astype(jnp.float32)[:, :, None, :], axis=-1)) * inv_root
    slots = jnp.arange(key_cache.shape[2], dtype=jnp.int32)
    visible = (slots[None, :] < lengths[:, None])[:, None, None, :]
    masked = jnp.where(visible, scores, -1e+30)
    peak = jnp.maximum(lax.optimization_barrier(jnp.max(masked, axis=-1)), self_score)
    weights = jnp.where(visible, jnp.exp(masked - peak[..., None]), 0.0)
    self_weight = jnp.exp(self_score - peak)
    denominator = lax.optimization_barrier(jnp.sum(weights, axis=-1)) + self_weight
    weights_bf = (weights / denominator[..., None]).astype(jnp.bfloat16)
    self_bf = (self_weight / denominator).astype(jnp.bfloat16)
    mixture = jnp.einsum('bkgc,bkcd->bkgd', weights_bf.astype(jnp.float32), cached_value_rows.astype(jnp.float32))
    mixture = mixture + self_bf.astype(jnp.float32)[..., None] * new_value.astype(jnp.float32)[:, :, None, :]
    attended = mixture.reshape(row_count, -1).astype(jnp.bfloat16)
    return (attended, new_key, new_value)

def reference(master_qo, master_kv, moment1_qo, moment1_kv, moment2_qo, moment2_kv, grad_qo, grad_kv, hidden, norm_gain, qk_gain, key_cache, cached_value_rows, lengths):
    grand_total = jnp.sum(grad_qo * grad_qo) + jnp.sum(grad_kv * grad_kv)
    clip_factor = jnp.minimum(1.0, clip_limit / (jnp.sqrt(grand_total) + eps_norm))
    fresh_qo = adam_update(master_qo, moment1_qo, moment2_qo, grad_qo, clip_factor)
    fresh_kv = adam_update(master_kv, moment1_kv, moment2_kv, grad_kv, clip_factor)
    weights_qo = fresh_qo[0].astype(jnp.bfloat16)
    weights_kv = fresh_kv[0].astype(jnp.bfloat16)
    normed = root_scale(hidden.astype(jnp.float32), norm_gain).astype(jnp.bfloat16)
    queries = jnp.dot(normed, weights_qo[0], preferred_element_type=jnp.float32)
    key_new = jnp.dot(normed, weights_kv[0], preferred_element_type=jnp.float32)
    value_new = jnp.dot(normed, weights_kv[1], preferred_element_type=jnp.float32)
    attended, new_key, new_value = attend(queries, key_new, value_new, qk_gain, key_cache, cached_value_rows, lengths)
    row_terms = lax.dot_general(attended, weights_qo[1], (((1,), (1,)), ((), ())), preferred_element_type=jnp.float32)
    new_hidden = (hidden.astype(jnp.float32) + row_terms).astype(jnp.bfloat16)
    return (fresh_qo[0], fresh_kv[0], fresh_qo[1], fresh_kv[1], fresh_qo[2], fresh_kv[2], new_hidden, new_key, new_value)
```

```python
import functools
import math

import jax
import jax.numpy as jnp
from jax import lax
from jax.experimental import pallas as pl
from jax.experimental.pallas import tpu as pltpu
from jax.sharding import PartitionSpec as P

clip_limit = 1.0
beta_one = 0.9
beta_two = 0.95
learn_rate = 0.01
decay_rate = 0.1
adam_step = 10.0
eps_adam = 1e-08
eps_norm = 1e-06
rope_base = 1000000.0
kernel_vmem = 48 * 1024 * 1024

F32 = jnp.float32
BF16 = jnp.bfloat16
ANY = pl.BlockSpec(memory_space=pl.ANY)


def adam_math(master, moment_one, moment_two, gradient, clip_factor):
    clipped = gradient * clip_factor
    moment_one = beta_one * moment_one + (1.0 - beta_one) * clipped
    moment_two = beta_two * moment_two + (1.0 - beta_two) * clipped * clipped
    fix_one = 1.0 - beta_one**adam_step
    fix_two = 1.0 - beta_two**adam_step
    root = jnp.sqrt(moment_two * (1.0 / fix_two)) + eps_adam
    step_size = moment_one * (1.0 / fix_one) / root
    master = master - learn_rate * (step_size + decay_rate * master)
    return (master, moment_one, moment_two)


def xor_perm(count, mask):
    return [(i, i ^ mask) for i in range(count)]


def xor_order(blocks, mask):
    count = blocks.shape[0]
    bit = 1
    while bit < count:
        pairs = blocks.reshape((count // (2 * bit), 2, bit) + blocks.shape[1:])
        swapped = jnp.flip(pairs, axis=1).reshape(blocks.shape)
        blocks = jnp.where((mask & bit) != 0, swapped, blocks)
        bit *= 2
    return blocks


def member_order(slabs, member):
    return xor_order(jnp.stack([slabs[-1]] + list(slabs[:-1])), member)


def row_parts(rows):
    return 2 if rows % 32 == 0 else 1


def slab_spec(place, parts, block_rows, width):
    def index(i, r, _):
        moving = jnp.where(i == place, r, parts - 1)
        return (jnp.where(i < place, 0, moving), 0)

    return pl.BlockSpec((block_rows, width), index)


def input_proj_kernel(members, group, head_dim, me_ref, clip_ref, *refs):
    ins, rest = refs[:8], refs[8:]
    rest = rest[len(rest) - 6 - members:]
    outs, slabs = rest[:6], rest[6:]
    clip = clip_ref[0, 0]
    fresh_q = adam_math(ins[0][0], ins[2][0], ins[4][0], ins[6][0], clip)
    fresh_k = adam_math(ins[1][0], ins[3][0], ins[5][0], ins[7][0], clip)
    fresh_v = adam_math(ins[1][1], ins[3][1], ins[5][1], ins[7][1], clip)
    for n in range(3):
        outs[2 * n][0] = fresh_q[n]
        outs[2 * n + 1][0] = fresh_k[n]
        outs[2 * n + 1][1] = fresh_v[n]
    for place in range(members):

        @pl.when(pl.program_id(0) == place)
        def _(place=place):
            slab = slabs[place]
            slab[:, :group] = fresh_q[0].astype(BF16)
            slab[:, group : group + head_dim] = fresh_k[0].astype(BF16)
            slab[:, group + head_dim :] = fresh_v[0].astype(BF16)


def output_proj_kernel(members, me_ref, clip_ref, *refs):
    ins, rest = refs[:4], refs[4:]
    rest = rest[len(rest) - 3 - members:]
    outs, slabs = rest[:3], rest[3:]
    fresh = adam_math(ins[0][0], ins[1][0], ins[2][0], ins[3][0], clip_ref[0, 0])
    for n in range(3):
        outs[n][0] = fresh[n]
    for place in range(members):

        @pl.when(pl.program_id(0) == place)
        def _(place=place):
            slabs[place][...] = fresh[0].astype(BF16)


def update_input_proj(head, heads, members, me, clip, qo, kv, earlier):
    rows = qo[0].shape[1]
    kv_total = heads * members
    group = qo[0].shape[2] // kv_total
    head_dim = kv[0].shape[2] // kv_total
    parts = row_parts(rows)
    block_rows = rows // parts

    def column(i, me_ref):
        return (me_ref[0] ^ ((i + 1) % members)) * heads + head

    qo_spec = pl.BlockSpec((1, block_rows, group), lambda i, r, m: (0, r, column(i, m)))
    kv_spec = pl.BlockSpec((2, block_rows, head_dim), lambda i, r, m: (0, r, column(i, m)))
    width = group + 2 * head_dim
    ins = [x for pair in zip(qo, kv) for x in pair]
    shapes = [jax.ShapeDtypeStruct(x.shape, F32) for x in ins[:6]]
    slabs = [jax.ShapeDtypeStruct((rows, width), BF16)] * members
    aliases = {}
    if earlier is not None:
        aliases = {10 + n: n for n in range(6)}
    earlier = [] if earlier is None else list(earlier)
    count = rows * members * (group + 2 * head_dim)
    results = pl.pallas_call(
        functools.partial(input_proj_kernel, members, group, head_dim),
        grid_spec=pltpu.PrefetchScalarGridSpec(
            num_scalar_prefetch=1,
            grid=(members, parts),
            in_specs=[pl.BlockSpec(memory_space=pltpu.SMEM)]
            + [qo_spec, kv_spec] * 4
            + [ANY] * len(earlier),
            out_specs=[qo_spec, kv_spec] * 3
            + [slab_spec(n, parts, block_rows, width) for n in range(members)],
        ),
        out_shape=shapes + slabs,
        input_output_aliases=aliases,
        compiler_params=pltpu.CompilerParams(vmem_limit_bytes=kernel_vmem),
        cost_estimate=pl.CostEstimate(
            flops=20 * count, bytes_accessed=30 * count, transcendentals=2 * count
        ),
    )(me, clip, *ins, *earlier)
    return results[:6], results[6:]


def update_output_proj(members, me, clip, qo, earlier):
    rows = qo[0].shape[1]
    width = qo[0].shape[2] // members
    parts = row_parts(rows)
    block_rows = rows // parts

    def column(i, me_ref):
        return me_ref[0] ^ ((i + 1) % members)

    spec = pl.BlockSpec((1, block_rows, width), lambda i, r, m: (1, r, column(i, m)))
    count = rows * members * width
    results = pl.pallas_call(
        functools.partial(output_proj_kernel, members),
        grid_spec=pltpu.PrefetchScalarGridSpec(
            num_scalar_prefetch=1,
            grid=(members, parts),
            in_specs=[pl.BlockSpec(memory_space=pltpu.SMEM)] + [spec] * 4 + [ANY] * 3,
            out_specs=[spec] * 3 + [slab_spec(n, parts, block_rows, width) for n in range(members)],
        ),
        out_shape=[jax.ShapeDtypeStruct(x.shape, F32) for x in qo[:3]]
        + [jax.ShapeDtypeStruct((rows, width), BF16)] * members,
        input_output_aliases={6 + n: n for n in range(3)},
        compiler_params=pltpu.CompilerParams(vmem_limit_bytes=kernel_vmem),
        cost_estimate=pl.CostEstimate(
            flops=20 * count, bytes_accessed=30 * count, transcendentals=2 * count
        ),
    )(me, clip, *qo, *earlier)
    return results[:3], results[3:]


def project_kernel(members, me_ref, x_ref, *refs):
    slabs, (send_ref, keep_ref, weight) = refs[:members], refs[members:]
    rows = slabs[0].shape[0]

    @pl.when(pl.program_id(0) == 0)
    def _():
        for place in range(members):
            owner = me_ref[0] ^ ((place + 1) % members)
            start = pl.multiple_of(owner * rows, rows)
            weight[pl.ds(start, rows), :] = slabs[place][...]

    part = jnp.dot(x_ref[0], weight[...], preferred_element_type=F32)

    @pl.when(pl.program_id(0) == 0)
    def _():
        send_ref[...] = part.astype(BF16)

    @pl.when(pl.program_id(0) == 1)
    def _():
        keep_ref[...] = part


def project(me, x, slabs):
    members = len(slabs)
    _, rows, depth = x.shape
    width = slabs[0].shape[1]
    if slabs[0].shape[0] % 16:
        weight = member_order(slabs, me[0]).reshape(depth, width)
        part = jnp.dot(x, weight, preferred_element_type=F32)
        return part[0].astype(BF16), part[1]
    whole = pl.BlockSpec(slabs[0].shape, lambda i, m: (0, 0))
    out = pl.BlockSpec((rows, width), lambda i, m: (0, 0))
    return pl.pallas_call(
        functools.partial(project_kernel, members),
        grid_spec=pltpu.PrefetchScalarGridSpec(
            num_scalar_prefetch=1,
            grid=(2,),
            in_specs=[pl.BlockSpec((1, rows, depth), lambda i, m: (i, 0, 0))] + [whole] * members,
            out_specs=[out, out],
            scratch_shapes=[pltpu.VMEM((depth, width), BF16)],
        ),
        out_shape=[
            jax.ShapeDtypeStruct((rows, width), BF16),
            jax.ShapeDtypeStruct((rows, width), F32),
        ],
        compiler_params=pltpu.CompilerParams(vmem_limit_bytes=kernel_vmem),
        cost_estimate=pl.CostEstimate(
            flops=4 * rows * depth * width, bytes_accessed=2 * 4 * rows * width, transcendentals=0
        ),
    )(me, x, *slabs)


def expand_kernel(members, zones, me_ref, core_ref, *refs):
    att, refs = refs[:zones], refs[zones:]
    slabs, refs = refs[: 2 * members], refs[2 * members :]
    outs, (weight, total) = refs[:members], refs[members:]
    rows = slabs[0].shape[0]
    row_count = att[0].shape[0]
    share = row_count // members
    for other in range(2):
        for place in range(members):
            owner = (core_ref[0] ^ other) * members + (me_ref[0] ^ ((place + 1) % members))
            start = pl.multiple_of(owner * rows, rows)
            weight[pl.ds(start, rows), :] = slabs[other * members + place][...]
    stacked = jnp.concatenate([a[...] for a in att], axis=0)
    part = lax.dot_general(
        stacked, weight[...], (((1,), (1,)), ((), ())), preferred_element_type=F32
    )
    for zone in range(zones):
        for member in range(members):
            first = zone * row_count + member * share
            total[member, zone * share : (zone + 1) * share, :] = part[first : first + share, :]
    for mask in range(members):
        outs[mask][...] = total[me_ref[0] ^ mask]


def expand(me, core, att, slabs):
    zones, members = len(att), len(slabs) // 2
    row_count, depth = att[0].shape
    rows = slabs[0].shape[0]
    width = 2 * members * rows
    share = zones * row_count // members
    if rows % 16:
        halves = jnp.stack([member_order(slabs[:members], me[0]), member_order(slabs[members:], me[0])])
        weight = xor_order(halves, core[0]).reshape(width, depth)
        part = lax.dot_general(
            jnp.stack(att), weight, (((2,), (1,)), ((), ())), preferred_element_type=F32
        )
        part = part.reshape(zones, members, row_count // members, width).transpose(1, 0, 2, 3)
        part = xor_order(part, me[0]).reshape(members, share, width)
        return [part[k] for k in range(members)]
    vmem = pl.BlockSpec(memory_space=pltpu.VMEM)
    smem = pl.BlockSpec(memory_space=pltpu.SMEM)
    return pl.pallas_call(
        functools.partial(expand_kernel, members, zones),
        in_specs=[smem, smem] + [vmem] * (zones + 2 * members),
        out_specs=[vmem] * members,
        scratch_shapes=[
            pltpu.VMEM((width, depth), BF16),
            pltpu.VMEM((members, share, width), F32),
        ],
        out_shape=[jax.ShapeDtypeStruct((share, width), F32)] * members,
        compiler_params=pltpu.CompilerParams(vmem_limit_bytes=kernel_vmem),
        cost_estimate=pl.CostEstimate(
            flops=2 * zones * row_count * depth * width,
            bytes_accessed=2 * width * depth,
            transcendentals=0,
        ),
    )(me, core, *att, *slabs)


def root_scale(values, gain_vec):
    mean_square = jnp.mean(values * values, axis=-1, keepdims=True)
    return values * lax.rsqrt(mean_square + eps_norm) * gain_vec


def rotate(values, positions):
    half_dim = values.shape[-1] // 2
    frequency = rope_base ** (-(jnp.arange(half_dim, dtype=F32) * 2.0) / values.shape[-1])
    angles = positions.astype(F32)[:, None] * frequency[None, :]
    cosine = jnp.cos(angles)[:, None, :]
    sine_part = jnp.sin(angles)[:, None, :]
    first_half = values[..., :half_dim]
    second = values[..., half_dim:]
    return jnp.concatenate(
        [first_half * cosine - second * sine_part, second * cosine + first_half * sine_part],
        axis=-1,
    )


def attend(queries, key_new, value_new, qk_gain, key_cache, cached_value_rows, lengths):
    row_count = queries.shape[0]
    kv_heads = key_cache.shape[1]
    head_dim = key_cache.shape[-1]
    queries = queries.reshape(row_count, -1, head_dim)
    key_new = key_new.reshape(row_count, kv_heads, head_dim)
    rotated = rotate(root_scale(queries, qk_gain[0]), lengths).astype(BF16)
    new_key = rotate(root_scale(key_new, qk_gain[1]), lengths).astype(BF16)
    new_value = value_new.reshape(row_count, kv_heads, head_dim).astype(BF16)
    group_size = rotated.shape[1] // kv_heads
    grouped = rotated.reshape(row_count, kv_heads, group_size, head_dim)
    inv_root = 1.0 / math.sqrt(head_dim)
    scores = (
        jnp.einsum("bkgd,bkcd->bkgc", grouped, key_cache, preferred_element_type=F32) * inv_root
    )
    self_score = (
        jnp.sum(grouped.astype(F32) * new_key.astype(F32)[:, :, None, :], axis=-1) * inv_root
    )
    slots = jnp.arange(key_cache.shape[2], dtype=jnp.int32)
    visible = (slots[None, :] < lengths[:, None])[:, None, None, :]
    masked = jnp.where(visible, scores, -1e30)
    peak = jnp.maximum(jnp.max(masked, axis=-1), self_score)
    weights = jnp.where(visible, jnp.exp(masked - peak[..., None]), 0.0)
    self_weight = jnp.exp(self_score - peak)
    denominator = jnp.sum(weights, axis=-1) + self_weight
    weights_bf = (weights / denominator[..., None]).astype(BF16)
    self_bf = (self_weight / denominator).astype(BF16)
    mixture = jnp.einsum(
        "bkgc,bkcd->bkgd", weights_bf, cached_value_rows, preferred_element_type=F32
    )
    mixture = mixture + self_bf.astype(F32)[..., None] * new_value.astype(F32)[:, :, None, :]
    attended = mixture.reshape(row_count, -1).astype(BF16)
    return (attended, new_key, new_value)


def local(
    master_qo,
    master_kv,
    moment1_qo,
    moment1_kv,
    moment2_qo,
    moment2_kv,
    grad_qo,
    grad_kv,
    hidden,
    norm_gain,
    qk_gain,
    key_cache,
    cached_value_rows,
    lengths,
):
    shards, members = lax.axis_size("fsdp"), lax.axis_size("tp")
    zones = shards // 2
    shard, member = lax.axis_index("fsdp"), lax.axis_index("tp")
    me = member.astype(jnp.int32).reshape(1)
    core = (shard & 1).astype(jnp.int32).reshape(1)
    own_rows, width = hidden.shape
    rows = master_qo.shape[1]
    slab_depth = members * rows
    heads = key_cache.shape[1]
    head_dim = key_cache.shape[3]
    group_rows = members * own_rows

    def swap_member(x, mask):
        return lax.ppermute(x, "tp", xor_perm(members, mask))

    def swap_zone(x, mask):
        return lax.ppermute(x, "fsdp", xor_perm(shards, 2 * mask))

    def swap_core(x):
        return lax.ppermute(x, "fsdp", xor_perm(shards, 1))

    local_squares = jnp.sum(grad_qo * grad_qo) + jnp.sum(grad_kv * grad_kv)
    spread = jnp.broadcast_to(local_squares, (shards * members, 1, 128))
    gathered = lax.all_to_all(spread, ("fsdp", "tp"), 0, 0)
    grand_total = jnp.sum(gathered[:, 0, 0])
    clip = jnp.minimum(1.0, clip_limit / (jnp.sqrt(grand_total) + eps_norm)).reshape(1, 1)

    normed_own = root_scale(hidden.astype(F32), norm_gain).astype(BF16)
    blocks = normed_own.reshape(own_rows, shards, slab_depth).transpose(1, 0, 2)
    mine = lax.all_to_all(blocks, "fsdp", 0, 0)
    parts = jnp.stack([mine] + [swap_member(mine, k) for k in range(1, members)])
    parts = xor_order(parts, member).transpose(1, 0, 2, 3)
    parts = xor_order(parts.reshape(shards, group_rows, slab_depth), shard)
    parts = parts.reshape(zones, 2, group_rows, slab_depth)
    x = jnp.flip(parts.transpose(1, 0, 2, 3), axis=0).reshape(2, zones * group_rows, slab_depth)

    qo = (master_qo, moment1_qo, moment2_qo, grad_qo)
    kv = (master_kv, moment1_kv, moment2_kv, grad_kv)
    fresh, received = None, []
    for head in range(heads):
        fresh, slabs = update_input_proj(head, heads, members, me, clip, qo, kv, fresh)
        received.append(
            [swap_member(slabs[n], n + 1) for n in range(members - 1)] + [slabs[members - 1]]
        )
    fresh_qo, slabs = update_output_proj(members, me, clip, qo, fresh[0::2])
    out_slabs = [swap_member(slabs[n], n + 1) for n in range(members - 1)] + [slabs[members - 1]]
    out_slabs = out_slabs + [swap_core(s) for s in out_slabs]

    summed = []
    for head in range(heads):
        send, keep = project(me, x, received[head])
        both = (keep + swap_core(send).astype(F32)).reshape(zones, group_rows, -1)
        total = both[0]
        for k in range(1, zones):
            total = total + swap_zone(both[k].astype(BF16), k).astype(F32)
        summed.append(total)
    q_width = summed[0].shape[1] - 2 * head_dim
    queries = jnp.concatenate([s[:, :q_width] for s in summed], axis=1)
    key_new = jnp.concatenate([s[:, q_width : q_width + head_dim] for s in summed], axis=1)
    value_new = jnp.concatenate([s[:, q_width + head_dim :] for s in summed], axis=1)
    attended, new_key, new_value = attend(
        queries, key_new, value_new, qk_gain, key_cache, cached_value_rows, lengths
    )

    att = [attended] + [swap_zone(attended, k) for k in range(1, zones)]
    shares = expand(me, core, att, out_slabs)
    own = shares[0]
    for k in range(1, members):
        own = own + swap_member(shares[k], k)
    own = own.reshape(zones, own_rows, 2 * slab_depth)
    pieces = jnp.stack([own[0]] + [swap_zone(own[k], k) for k in range(1, zones)])
    row_terms = xor_order(pieces, shard // 2).transpose(1, 0, 2).reshape(own_rows, width)
    new_hidden = (hidden.astype(F32) + row_terms).astype(BF16)
    return (
        fresh_qo[0],
        fresh[1],
        fresh_qo[1],
        fresh[3],
        fresh_qo[2],
        fresh[5],
        new_hidden,
        new_key,
        new_value,
    )


def solution(mesh):
    state = P(None, ("fsdp", "tp"), None)
    return jax.shard_map(
        local,
        mesh=mesh,
        in_specs=(
            state,
            state,
            state,
            state,
            state,
            state,
            state,
            state,
            P(("fsdp", "tp"), None),
            P(),
            P(),
            P("fsdp", "tp", None, None),
            P("fsdp", "tp", None, None),
            P("fsdp"),
        ),
        out_specs=(
            state,
            state,
            state,
            state,
            state,
            state,
            P(("fsdp", "tp"), None),
            P("fsdp", "tp", None),
            P("fsdp", "tp", None),
        ),
        check_vma=False,
    )
```

```python
import functools
import math

import jax
import jax.numpy as jnp
from jax import lax
from jax.experimental import pallas as pl
from jax.experimental.pallas import tpu as pltpu
from jax.sharding import PartitionSpec as P

clip_limit = 1.0
beta_one = 0.9
beta_two = 0.95
learn_rate = 0.01
decay_rate = 0.1
adam_step = 10.0
eps_adam = 1e-08
eps_norm = 1e-06
rope_base = 1000000.0
kernel_vmem = 24 * 1024 * 1024
wide_vmem = 32 * 1024 * 1024

F32 = jnp.float32
BF16 = jnp.bfloat16
ANY = pl.BlockSpec(memory_space=pl.ANY)
small_cost = pl.CostEstimate(flops=1024, bytes_accessed=1024, transcendentals=0)


def adam_math(master, moment_one, moment_two, gradient, clip_factor):
    clipped = gradient * clip_factor
    moment_one = beta_one * moment_one + (1.0 - beta_one) * clipped
    moment_two = beta_two * moment_two + (1.0 - beta_two) * clipped * clipped
    fix_one = 1.0 - beta_one**adam_step
    fix_two = 1.0 - beta_two**adam_step
    root = jnp.sqrt(moment_two * (1.0 / fix_two)) + eps_adam
    step_size = moment_one * (1.0 / fix_one) / root
    master = master - learn_rate * (step_size + decay_rate * master)
    return (master, moment_one, moment_two)


def in_hbm(x):
    return pltpu.with_memory_space_constraint(x, pltpu.HBM)


def xor_perm(count, mask):
    return [(i, i ^ mask) for i in range(count)]


def xor_order(blocks, mask):
    count = blocks.shape[0]
    bit = 1
    while bit < count:
        pairs = blocks.reshape((count // (2 * bit), 2, bit) + blocks.shape[1:])
        swapped = jnp.flip(pairs, axis=1).reshape(blocks.shape)
        blocks = jnp.where((mask & bit) != 0, swapped, blocks)
        bit *= 2
    return blocks


def clip_of(squares):
    total = jnp.sum(squares[:, 0, :], axis=0, keepdims=True)[:, :1]
    return jnp.minimum(1.0, clip_limit / (jnp.sqrt(total) + eps_norm))


def squares_kernel(qo_ref, kv_ref, out_ref, total):
    def folded(block):
        block = (block * block).reshape(-1, 8, block.shape[-1]).sum(0)
        lanes = total.shape[-1]
        return sum(block[:, n : n + lanes] for n in range(0, block.shape[-1], lanes))

    @pl.when(pl.program_id(0) == 0)
    def _():
        total[...] = folded(kv_ref[0]) + folded(kv_ref[1])

    total[...] += folded(qo_ref[0])

    @pl.when(pl.program_id(0) == pl.num_programs(0) - 1)
    def _():
        out_ref[...] = jnp.broadcast_to(jnp.sum(total[...]), out_ref.shape)


def local_squares(count, grad_qo, grad_kv):
    halves, rows, width = grad_qo.shape
    lanes = 1024 if width % 1024 == 0 and grad_kv.shape[2] % 1024 == 0 else 128
    return pl.pallas_call(
        squares_kernel,
        name="grad_squares",
        grid=(halves,),
        in_specs=[
            pl.BlockSpec((1, rows, width), lambda i: (i, 0, 0)),
            pl.BlockSpec(grad_kv.shape, lambda i: (0, 0, 0)),
        ],
        out_specs=pl.BlockSpec((count, 1, 128), lambda i: (0, 0, 0)),
        out_shape=jax.ShapeDtypeStruct((count, 1, 128), F32),
        scratch_shapes=[pltpu.VMEM((8, lanes), F32)],
        compiler_params=pltpu.CompilerParams(vmem_limit_bytes=kernel_vmem),
        cost_estimate=small_cost,
    )(grad_qo, grad_kv)


def norm_kernel(shards, members, hidden_ref, gain_ref, out_ref):
    values = hidden_ref[...].astype(F32)
    mean_square = jnp.mean(values * values, axis=-1, keepdims=True)
    normed = (values * lax.rsqrt(mean_square + eps_norm) * gain_ref[...]).astype(BF16)
    depth = values.shape[1] // shards
    for shard in range(shards):
        for member in range(members):
            out_ref[shard * members + member] = normed[:, shard * depth : (shard + 1) * depth]


def norm_blocks(shards, members, hidden, gain):
    rows, width = hidden.shape
    return pl.pallas_call(
        functools.partial(norm_kernel, shards, members),
        name="norm_rows",
        out_shape=jax.ShapeDtypeStruct((shards * members, rows, width // shards), BF16),
        compiler_params=pltpu.CompilerParams(vmem_limit_bytes=kernel_vmem // 2),
        cost_estimate=small_cost,
    )(hidden, gain.reshape(1, width))


def tie_kernel(*refs):
    pass


def tie(x, *deps):
    return pl.pallas_call(
        tie_kernel,
        name="tie",
        in_specs=[ANY] * (1 + len(deps)),
        out_specs=ANY,
        out_shape=pltpu.HBM(x.shape, x.dtype),
        input_output_aliases={0: 0},
        compiler_params=pltpu.CompilerParams(has_side_effects=True),
        cost_estimate=small_cost,
    )(x, *deps)


def input_proj_kernel(stacked, count, group, head_dim, me_ref, squares_ref, *refs):
    ins, outs, slabs = refs[:8], refs[-6 - count : -count], refs[-count:]
    clip = clip_of(squares_ref)
    fresh_q = adam_math(ins[0][0], ins[2][0], ins[4][0], ins[6][0], clip)
    fresh_k = adam_math(ins[1][0], ins[3][0], ins[5][0], ins[7][0], clip)
    fresh_v = adam_math(ins[1][1], ins[3][1], ins[5][1], ins[7][1], clip)
    for n in range(3):
        outs[2 * n][0] = fresh_q[n]
        outs[2 * n + 1][0] = fresh_k[n]
        outs[2 * n + 1][1] = fresh_v[n]

    def fill(slab):
        slab[:, :group] = fresh_q[0].astype(BF16)
        slab[:, group : group + head_dim] = fresh_k[0].astype(BF16)
        slab[:, group + head_dim :] = fresh_v[0].astype(BF16)

    if stacked:
        fill(slabs[0].at[0])
        return
    for place in range(count):

        @pl.when(pl.program_id(0) == place)
        def _(place=place):
            fill(slabs[place])


def update_input_proj(head, heads, members, first, count, me, squares, qo, kv, earlier):
    rows = qo[0].shape[1]
    kv_total = heads * members
    group = qo[0].shape[2] // kv_total
    head_dim = kv[0].shape[2] // kv_total
    width = group + 2 * head_dim

    def column(i, me_ref):
        member = i if first is None else me_ref[0] ^ ((first + i) % members)
        return member * heads + head

    qo_spec = pl.BlockSpec((1, rows, group), lambda i, m: (0, 0, column(i, m)))
    kv_spec = pl.BlockSpec((2, rows, head_dim), lambda i, m: (0, 0, column(i, m)))
    earlier = [] if earlier is None else list(earlier)
    ins = [x for pair in zip(qo, kv) for x in pair]
    if first is None:
        slabs = [pltpu.HBM((members, rows, width), BF16)]
        slab_specs = [pl.BlockSpec((1, rows, width), lambda i, m: (i, 0, 0))]
    else:
        slabs = [pltpu.HBM((rows, width), BF16)] * count
        slab_specs = [pl.BlockSpec((rows, width), lambda i, m: (0, 0))] * count
    results = pl.pallas_call(
        functools.partial(input_proj_kernel, first is None, len(slabs), group, head_dim),
        name="adam_in",
        grid_spec=pltpu.PrefetchScalarGridSpec(
            num_scalar_prefetch=1,
            grid=(count,),
            in_specs=[pl.BlockSpec(squares.shape, lambda i, m: (0, 0, 0))]
            + [qo_spec, kv_spec] * 4
            + [ANY] * len(earlier),
            out_specs=[qo_spec, kv_spec] * 3 + slab_specs,
        ),
        out_shape=[pltpu.HBM(x.shape, F32) for x in ins[:6]] + slabs,
        input_output_aliases={10 + n: n for n in range(len(earlier))},
        compiler_params=pltpu.CompilerParams(vmem_limit_bytes=wide_vmem),
        cost_estimate=small_cost,
    )(me, squares, *ins, *earlier)
    return results[:6], results[6:]


def output_proj_kernel(squares_ref, *refs):
    ins, (*outs, slab) = refs[:4], refs[-4:]
    clip = clip_of(squares_ref)
    fresh = adam_math(ins[0][0], ins[1][0], ins[2][0], ins[3][0], clip)
    for n in range(3):
        outs[n][0] = fresh[n]
    width = slab.shape[2]
    for member in range(slab.shape[0]):
        slab[member] = fresh[0][:, member * width : (member + 1) * width].astype(BF16)


def update_output_proj(members, squares, qo, earlier, deps):
    rows = qo[0].shape[1]
    width = qo[0].shape[2] // members
    half = members // 2
    untouched = list(earlier) + list(deps)
    spec = pl.BlockSpec((1, rows, half * width), lambda i: (1, 0, i))
    return pl.pallas_call(
        output_proj_kernel,
        name="adam_out",
        grid=(2,),
        in_specs=[pl.BlockSpec(squares.shape, lambda i: (0, 0, 0))]
        + [spec] * 4
        + [ANY] * len(untouched),
        out_specs=[spec] * 3 + [pl.BlockSpec((half, rows, width), lambda i: (i, 0, 0))],
        out_shape=[pltpu.HBM(x.shape, F32) for x in qo[:3]]
        + [pltpu.HBM((members, rows, width), BF16)],
        input_output_aliases={5 + n: n for n in range(len(earlier))},
        compiler_params=pltpu.CompilerParams(vmem_limit_bytes=2 * wide_vmem - kernel_vmem // 6),
        cost_estimate=small_cost,
    )(squares, *qo, *untouched)


def project_kernel(count, me_ref, shard_ref, x_ref, *refs):
    slabs, (send_ref, keep_ref, mine, other, *scratch) = refs[:count], refs[count:]
    weight = slabs[0]
    if count > 1:
        weight = scratch[0]
        rows = slabs[0].shape[0]
        for place in range(count):
            start = pl.multiple_of((me_ref[0] ^ place) * rows, rows)
            weight[pl.ds(start, rows), :] = slabs[place][...]
    shards, group_rows, _ = x_ref.shape
    for mask in range(shards):
        into = other if mask % 2 else mine
        start = mask // 2 * group_rows
        into[start : start + group_rows, :] = x_ref[shard_ref[0] ^ mask]
    send_ref[...] = jnp.dot(other[...], weight[...], preferred_element_type=F32).astype(BF16)
    keep_ref[...] = jnp.dot(mine[...], weight[...], preferred_element_type=F32)


def project(me, shard, x, slabs, deps):
    shards, group_rows, depth = x.shape
    rows, width = slabs[0].shape
    half = shards // 2 * group_rows
    if rows % 16 and len(slabs) > 1:
        slabs = [xor_order(jnp.stack(slabs), me[0]).reshape(depth, width)]
    count = len(slabs)
    vmem = pl.BlockSpec(memory_space=pltpu.VMEM)
    smem = pl.BlockSpec(memory_space=pltpu.SMEM)

    def body(me_ref, shard_ref, x_ref, *refs):
        project_kernel(count, me_ref, shard_ref, x_ref, *refs[:count], *refs[count + len(deps) :])

    scratch = [pltpu.VMEM((half, depth), BF16)] * 2
    if count > 1:
        scratch.append(pltpu.VMEM((depth, width), BF16))
    return pl.pallas_call(
        body,
        name="project",
        in_specs=[smem, smem] + [vmem] * (1 + count) + [ANY] * len(deps),
        out_specs=[vmem, vmem],
        scratch_shapes=scratch,
        out_shape=[pltpu.HBM((half, width), BF16), pltpu.HBM((half, width), F32)],
        compiler_params=pltpu.CompilerParams(vmem_limit_bytes=kernel_vmem),
        cost_estimate=small_cost,
    )(me, shard, x, *slabs, *deps)


def core_sum_kernel(zones, keep_ref, arrived_ref, *refs):
    own_ref, sends = refs[-zones], refs[len(refs) - zones + 1 :]
    rows = own_ref.shape[0]
    for zone in range(zones):
        span = pl.ds(zone * rows, rows)
        total = keep_ref[span, :] + arrived_ref[span, :].astype(F32)
        if zone == 0:
            own_ref[...] = total
        else:
            sends[zone - 1][...] = total.astype(BF16)


def core_sum(zones, keep, arrived, deps):
    rows, width = keep.shape[0] // zones, keep.shape[1]
    vmem = pl.BlockSpec(memory_space=pltpu.VMEM)
    return pl.pallas_call(
        functools.partial(core_sum_kernel, zones),
        name="core_sum",
        in_specs=[vmem, vmem] + [ANY] * len(deps),
        out_specs=[vmem] * zones,
        out_shape=[pltpu.HBM((rows, width), F32)]
        + [jax.ShapeDtypeStruct((rows, width), BF16)] * (zones - 1),
        compiler_params=pltpu.CompilerParams(vmem_limit_bytes=kernel_vmem),
        cost_estimate=small_cost,
    )(in_hbm(keep), arrived, *deps)


def attend_kernel(zones, *refs):
    lens_ref, cos_ref, sin_ref, gain_ref, key_ref, value_ref = refs[:6]
    parts = refs[6 : 6 + zones]
    out_ref, new_key_ref, new_value_ref, query, mixed = refs[-5:]
    head_dim = new_key_ref.shape[1]
    groups = query.shape[1]
    total = parts[0][...]
    for part in parts[1:]:
        total = total + part[...].astype(F32)
    cosine, sine = cos_ref[...], sin_ref[...]

    def placed(values, gain):
        mean_square = jnp.mean(values * values, axis=-1, keepdims=True)
        values = values * lax.rsqrt(mean_square + eps_norm) * gain
        return values * cosine + pltpu.roll(values, head_dim // 2, 1) * sine

    for group in range(groups):
        columns = total[:, group * head_dim : (group + 1) * head_dim]
        query[:, group, :] = placed(columns, gain_ref[0:1, :])
    new_key = placed(total[:, groups * head_dim : (groups + 1) * head_dim], gain_ref[1:2, :])
    new_key = new_key.astype(BF16)
    new_value = total[:, (groups + 1) * head_dim :].astype(BF16)
    new_key_ref[...] = new_key
    new_value_ref[...] = new_value
    inv_root = 1.0 / math.sqrt(head_dim)
    rotated = query[...].astype(BF16)
    scores = inv_root * lax.dot_general(
        rotated, key_ref[:, 0], (((2,), (2,)), ((0,), (0,))), preferred_element_type=F32
    )
    own_score = inv_root * jnp.sum(
        rotated.astype(F32) * new_key.astype(F32)[:, None, :], axis=-1, keepdims=True
    )
    slots = lax.broadcasted_iota(jnp.int32, scores.shape, 2)
    visible = slots < lens_ref[...][:, None, :]
    masked = jnp.where(visible, scores, -1e30)
    peak = jnp.maximum(jnp.max(masked, axis=-1, keepdims=True), own_score)
    weights = jnp.where(visible, jnp.exp(masked - peak), 0.0)
    own_weight = jnp.exp(own_score - peak)
    inverse = 1.0 / (jnp.sum(weights, axis=-1, keepdims=True) + own_weight)
    own_part = (own_weight * inverse).astype(BF16).astype(F32)
    mixed[...] = (
        lax.dot_general(
            (weights * inverse).astype(BF16),
            value_ref[:, 0],
            (((2,), (1,)), ((0,), (0,))),
            preferred_element_type=F32,
        )
        + own_part * new_value.astype(F32)[:, None, :]
    )
    for group in range(groups):
        out_ref[:, group * head_dim : (group + 1) * head_dim] = mixed[:, group, :].astype(BF16)


def attend(head, parts, lens, cosine, sine, qk_gain, cache, deps):
    rows, width = parts[0].shape
    slots, head_dim = cache[0].shape[2:]
    groups = width // head_dim - 2
    block = 16
    row_block = lambda columns: pl.BlockSpec((block, columns), lambda i: (i, 0))
    cache_block = pl.BlockSpec((block, 1, slots, head_dim), lambda i: (i, head, 0, 0))
    return pl.pallas_call(
        functools.partial(attend_kernel, len(parts)),
        name="attend",
        grid=(rows // block,),
        in_specs=[row_block(slots), row_block(head_dim), row_block(head_dim)]
        + [pl.BlockSpec((2, head_dim), lambda i: (0, 0)), cache_block, cache_block]
        + [row_block(width)] * len(parts)
        + [ANY] * len(deps),
        out_specs=[
            row_block(groups * head_dim),
            row_block(head_dim),
            row_block(head_dim),
        ],
        out_shape=[
            pltpu.HBM((rows, groups * head_dim), BF16),
            jax.ShapeDtypeStruct((rows, head_dim), BF16),
            jax.ShapeDtypeStruct((rows, head_dim), BF16),
        ],
        scratch_shapes=[pltpu.VMEM((block, groups, head_dim), F32)] * 2,
        compiler_params=pltpu.CompilerParams(vmem_limit_bytes=kernel_vmem),
        cost_estimate=small_cost,
    )(lens, cosine, sine, qk_gain, *cache, in_hbm(parts[0]), *parts[1:], *deps)


def stack_rows_kernel(count, *refs):
    parts, out, sems = refs[:count], refs[-2], refs[-1]
    rows = parts[0].shape[0]
    copies = [
        pltpu.make_async_copy(parts[n], out.at[pl.ds(n * rows, rows)], sems.at[n])
        for n in range(count)
    ]
    for copy in copies:
        copy.start()
    for copy in copies:
        copy.wait()


def stack_rows(parts, deps):
    rows, width = parts[0].shape
    return pl.pallas_call(
        functools.partial(stack_rows_kernel, len(parts)),
        name="stack_rows",
        in_specs=[ANY] * (len(parts) + len(deps)),
        out_specs=ANY,
        out_shape=pltpu.HBM((len(parts) * rows, width), BF16),
        scratch_shapes=[pltpu.SemaphoreType.DMA((len(parts),))],
        compiler_params=pltpu.CompilerParams(vmem_limit_bytes=kernel_vmem // 8),
        cost_estimate=small_cost,
    )(*parts, *deps)


def expand_kernel(members, heads, shard_ref, me_ref, *refs):
    att, refs = refs[: 2 * heads], refs[2 * heads :]
    slab, outs, total = refs[0], refs[1 : 1 + members], refs[-1]
    depth = att[0].shape[1]
    shards, share, _ = outs[0].shape
    zones = shards // 2
    for other in range(2):
        part = None
        for head in range(heads):
            term = lax.dot_general(
                att[2 * head + other][...],
                slab[:, head * depth : (head + 1) * depth],
                (((1,), (1,)), ((), ())),
                preferred_element_type=F32,
            )
            part = term if part is None else part + term
        for zone in range(zones):
            shard = shard_ref[0] ^ (2 * zone + other)
            for member in range(members):
                first = (zone * members + member) * share
                total[member, shard] = part[first : first + share, :]
    for mask in range(members):
        outs[mask][...] = total[me_ref[0] ^ mask].astype(outs[mask].dtype)


def expand(shard, me, att, slab):
    heads, members = len(att) // 2, lax.axis_size("tp")
    shards = lax.axis_size("fsdp")
    width = slab.shape[0]
    share = 2 * att[0].shape[0] // (shards * members)
    dtypes = [F32] + [BF16] * (members - 1)
    vmem = pl.BlockSpec(memory_space=pltpu.VMEM)
    smem = pl.BlockSpec(memory_space=pltpu.SMEM)
    return pl.pallas_call(
        functools.partial(expand_kernel, members, heads),
        name="expand",
        in_specs=[smem, smem] + [vmem] * (2 * heads + 1),
        out_specs=[vmem] * members,
        scratch_shapes=[pltpu.VMEM((members, shards, share, width), F32)],
        out_shape=[jax.ShapeDtypeStruct((shards, share, width), dtype) for dtype in dtypes],
        compiler_params=pltpu.CompilerParams(vmem_limit_bytes=kernel_vmem),
        cost_estimate=small_cost,
    )(shard, me, *[in_hbm(a) for a in att], slab)


def member_sum_kernel(*refs):
    total = refs[0][...]
    for share in refs[1:-1]:
        total = total + share[...].astype(F32)
    refs[-1][...] = total.astype(BF16)


def member_sum(shares):
    return pl.pallas_call(
        member_sum_kernel,
        name="member_sum",
        out_shape=jax.ShapeDtypeStruct(shares[0].shape, BF16),
        compiler_params=pltpu.CompilerParams(vmem_limit_bytes=kernel_vmem),
        cost_estimate=small_cost,
    )(*shares)


def finish_kernel(hidden_ref, pieces_ref, out_ref):
    row_terms = jnp.concatenate([pieces_ref[n] for n in range(pieces_ref.shape[0])], axis=1)
    out_ref[...] = (hidden_ref[...].astype(F32) + row_terms.astype(F32)).astype(BF16)


def finish(hidden, pieces):
    return pl.pallas_call(
        finish_kernel,
        name="finish",
        out_shape=jax.ShapeDtypeStruct(hidden.shape, BF16),
        compiler_params=pltpu.CompilerParams(vmem_limit_bytes=kernel_vmem),
        cost_estimate=small_cost,
    )(hidden, pieces)


def angles(positions, head_dim, slots):
    half_dim = head_dim // 2
    frequency = rope_base ** (-(jnp.arange(half_dim, dtype=F32) * 2.0) / head_dim)
    turned = positions.astype(F32)[:, None] * frequency[None, :]
    cosine, sine = jnp.cos(turned), jnp.sin(turned)
    lens = jnp.broadcast_to(positions[:, None], (positions.shape[0], slots))
    return (
        jnp.concatenate([cosine, cosine], axis=1),
        jnp.concatenate([-sine, sine], axis=1),
        lens,
    )


def local(
    master_qo,
    master_kv,
    moment1_qo,
    moment1_kv,
    moment2_qo,
    moment2_kv,
    grad_qo,
    grad_kv,
    hidden,
    norm_gain,
    qk_gain,
    key_cache,
    cached_value_rows,
    lengths,
):
    shards, members = lax.axis_size("fsdp"), lax.axis_size("tp")
    zones = shards // 2
    shard, member = lax.axis_index("fsdp"), lax.axis_index("tp")
    me = member.astype(jnp.int32).reshape(1)
    shard = shard.astype(jnp.int32).reshape(1)
    heads, slots, head_dim = key_cache.shape[1:]

    def swap_member(x, mask):
        return lax.ppermute(x, "tp", xor_perm(members, mask))

    def swap_zone(x, mask):
        return lax.ppermute(x, "fsdp", xor_perm(shards, 2 * mask))

    def swap_core(x):
        return lax.ppermute(x, "fsdp", xor_perm(shards, 1))

    qo = [in_hbm(x) for x in (master_qo, moment1_qo, moment2_qo, grad_qo)]
    kv = [in_hbm(x) for x in (master_kv, moment1_kv, moment2_kv, grad_kv)]
    cache = [in_hbm(key_cache), in_hbm(cached_value_rows)]

    blocks = norm_blocks(shards, members, hidden, norm_gain)
    x = lax.all_to_all(blocks, ("fsdp", "tp"), 0, 0)
    x = x.reshape(shards, -1, blocks.shape[2])

    spread = local_squares(shards * members, qo[3], kv[3])
    squares = lax.all_to_all(spread, ("fsdp", "tp"), 0, 0)

    fresh, slabs = update_input_proj(0, heads, members, 1, members - 1, me, squares, qo, kv, None)
    slabs = [list(slabs)]
    for head in range(1, heads):
        fresh, slab = update_input_proj(
            head, heads, members, None, members, me, squares, qo, kv, fresh
        )
        slabs.append(slab[0])
    fresh, slab = update_input_proj(0, heads, members, 0, 1, me, squares, qo, kv, fresh)
    slabs[0] = list(slab) + slabs[0]
    fresh_kv = fresh[1::2]
    fresh_qo = fresh[0::2]

    cosine, sine, lens = angles(lengths, head_dim, slots)
    parts, latest = [], [slabs[0][0]]
    for head in range(heads):
        if head == 0:
            weights = slabs[0][:1]
            weights += [swap_member(slabs[0][k], k) for k in range(1, members)]
        else:
            weights = lax.all_to_all(tie(slabs[head], send), "tp", 0, 0)
            weights = [weights.reshape(-1, weights.shape[2])]
        send, keep = project(me, shard, x, weights, latest)
        own, *sends = core_sum(zones, keep, swap_core(send), [])
        arrived = [swap_zone(sends[k - 1], k) for k in range(1, zones)]
        parts.append([own] + arrived)
        if head == 0:
            fresh_qo = update_output_proj(members, squares, qo, fresh_qo, sends)
            latest = [fresh_qo[3]] + arrived
    new_keys, new_values, attended = [], [], []
    latest = parts[-1][1:2]
    for head in range(heads):
        rows_out, new_key, new_value = attend(
            head, parts[head], lens, cosine, sine, qk_gain, cache, latest
        )
        new_keys.append(new_key)
        new_values.append(new_value)
        gathered = [rows_out] + [swap_zone(rows_out, k) for k in range(1, zones)]
        latest = gathered[1:2]
        attended.append(stack_rows(gathered, []))
    attended = [x for rows in attended for x in (rows, swap_core(rows))]
    out_slab = lax.all_to_all(tie(fresh_qo[3], send), "tp", 0, 0)
    out_slab = out_slab.reshape(-1, out_slab.shape[2])

    shares = expand(shard, me, attended, out_slab)
    shares = [shares[0]] + [swap_member(shares[k], k) for k in range(1, members)]
    pieces = lax.all_to_all(member_sum(shares), "fsdp", 0, 0)
    new_hidden = finish(hidden, pieces)
    return (
        fresh_qo[0],
        fresh_kv[0],
        fresh_qo[1],
        fresh_kv[1],
        fresh_qo[2],
        fresh_kv[2],
        new_hidden,
        jnp.stack(new_keys, axis=1),
        jnp.stack(new_values, axis=1),
    )


def solution(mesh):
    state = P(None, ("fsdp", "tp"), None)
    return jax.shard_map(
        local,
        mesh=mesh,
        in_specs=(
            state,
            state,
            state,
            state,
            state,
            state,
            state,
            state,
            P(("fsdp", "tp"), None),
            P(),
            P(),
            P("fsdp", "tp", None, None),
            P("fsdp", "tp", None, None),
            P("fsdp"),
        ),
        out_specs=(
            state,
            state,
            state,
            state,
            state,
            state,
            P(("fsdp", "tp"), None),
            P("fsdp", "tp", None),
            P("fsdp", "tp", None),
        ),
        check_vma=False,
    )
```

```python
import functools
import math

import jax
import jax.numpy as jnp
from jax import lax
from jax.experimental import pallas as pl
from jax.experimental.pallas import tpu as pltpu
from jax.sharding import PartitionSpec as P

clip_limit = 1.0
beta_one = 0.9
beta_two = 0.95
learn_rate = 0.01
decay_rate = 0.1
adam_step = 10.0
eps_adam = 1e-08
eps_norm = 1e-06
rope_base = 1000000.0
kernel_vmem = 24 * 1024 * 1024
wide_vmem = 32 * 1024 * 1024

F32 = jnp.float32
BF16 = jnp.bfloat16
ANY = pl.BlockSpec(memory_space=pl.ANY)
small_cost = pl.CostEstimate(flops=1024, bytes_accessed=1024, transcendentals=0)


def adam_math(master, moment_one, moment_two, gradient, clip_factor):
    clipped = gradient * clip_factor
    moment_one = beta_one * moment_one + (1.0 - beta_one) * clipped
    moment_two = beta_two * moment_two + (1.0 - beta_two) * clipped * clipped
    fix_one = 1.0 - beta_one**adam_step
    fix_two = 1.0 - beta_two**adam_step
    root = jnp.sqrt(moment_two * (1.0 / fix_two)) + eps_adam
    step_size = moment_one * (1.0 / fix_one) / root
    master = master - learn_rate * (step_size + decay_rate * master)
    return (master, moment_one, moment_two)


def in_hbm(x):
    return pltpu.with_memory_space_constraint(x, pltpu.HBM)


def xor_perm(count, mask):
    return [(i, i ^ mask) for i in range(count)]


def xor_order(blocks, mask):
    count = blocks.shape[0]
    bit = 1
    while bit < count:
        pairs = blocks.reshape((count // (2 * bit), 2, bit) + blocks.shape[1:])
        swapped = jnp.flip(pairs, axis=1).reshape(blocks.shape)
        blocks = jnp.where((mask & bit) != 0, swapped, blocks)
        bit *= 2
    return blocks


def clip_of(squares):
    total = jnp.sum(squares[:, 0, :], axis=0, keepdims=True)[:, :1]
    return jnp.minimum(1.0, clip_limit / (jnp.sqrt(total) + eps_norm))


def squares_kernel(qo_ref, kv_ref, out_ref, total):
    def folded(block):
        block = (block * block).reshape(-1, 8, block.shape[-1]).sum(0)
        lanes = total.shape[-1]
        return sum(block[:, n : n + lanes] for n in range(0, block.shape[-1], lanes))

    @pl.when(pl.program_id(0) == 0)
    def _():
        total[...] = folded(kv_ref[0]) + folded(kv_ref[1])

    total[...] += folded(qo_ref[0])

    @pl.when(pl.program_id(0) == pl.num_programs(0) - 1)
    def _():
        out_ref[...] = jnp.broadcast_to(jnp.sum(total[...]), out_ref.shape)


def local_squares(count, grad_qo, grad_kv):
    halves, rows, width = grad_qo.shape
    lanes = 1024 if width % 1024 == 0 and grad_kv.shape[2] % 1024 == 0 else 128
    return pl.pallas_call(
        squares_kernel,
        name="grad_squares",
        grid=(halves,),
        in_specs=[
            pl.BlockSpec((1, rows, width), lambda i: (i, 0, 0)),
            pl.BlockSpec(grad_kv.shape, lambda i: (0, 0, 0)),
        ],
        out_specs=pl.BlockSpec((count, 1, 128), lambda i: (0, 0, 0)),
        out_shape=jax.ShapeDtypeStruct((count, 1, 128), F32),
        scratch_shapes=[pltpu.VMEM((8, lanes), F32)],
        compiler_params=pltpu.CompilerParams(vmem_limit_bytes=kernel_vmem),
        cost_estimate=small_cost,
    )(grad_qo, grad_kv)


def norm_kernel(shards, members, hidden_ref, gain_ref, out_ref):
    values = hidden_ref[...].astype(F32)
    mean_square = jnp.mean(values * values, axis=-1, keepdims=True)
    normed = (values * lax.rsqrt(mean_square + eps_norm) * gain_ref[...]).astype(BF16)
    depth = values.shape[1] // shards
    for shard in range(shards):
        for member in range(members):
            out_ref[shard * members + member] = normed[:, shard * depth : (shard + 1) * depth]


def norm_blocks(shards, members, hidden, gain):
    rows, width = hidden.shape
    return pl.pallas_call(
        functools.partial(norm_kernel, shards, members),
        name="norm_rows",
        out_shape=jax.ShapeDtypeStruct((shards * members, rows, width // shards), BF16),
        compiler_params=pltpu.CompilerParams(vmem_limit_bytes=kernel_vmem // 2),
        cost_estimate=small_cost,
    )(hidden, gain.reshape(1, width))


def tie_kernel(*refs):
    pass


def tie(x, *deps):
    return pl.pallas_call(
        tie_kernel,
        name="tie",
        in_specs=[ANY] * (1 + len(deps)),
        out_specs=ANY,
        out_shape=pltpu.HBM(x.shape, x.dtype),
        input_output_aliases={0: 0},
        compiler_params=pltpu.CompilerParams(has_side_effects=True),
        cost_estimate=small_cost,
    )(x, *deps)


def input_proj_kernel(stacked, count, group, head_dim, me_ref, squares_ref, *refs):
    ins, outs, slabs = refs[:8], refs[-6 - count : -count], refs[-count:]
    clip = clip_of(squares_ref)
    fresh_q = adam_math(ins[0][0], ins[2][0], ins[4][0], ins[6][0], clip)
    fresh_k = adam_math(ins[1][0], ins[3][0], ins[5][0], ins[7][0], clip)
    fresh_v = adam_math(ins[1][1], ins[3][1], ins[5][1], ins[7][1], clip)
    for n in range(3):
        outs[2 * n][0] = fresh_q[n]
        outs[2 * n + 1][0] = fresh_k[n]
        outs[2 * n + 1][1] = fresh_v[n]

    def fill(slab):
        slab[:, :group] = fresh_q[0].astype(BF16)
        slab[:, group : group + head_dim] = fresh_k[0].astype(BF16)
        slab[:, group + head_dim :] = fresh_v[0].astype(BF16)

    if stacked:
        fill(slabs[0].at[0])
        return
    for place in range(count):

        @pl.when(pl.program_id(0) == place)
        def _(place=place):
            fill(slabs[place])


def update_input_proj(head, heads, members, first, count, me, squares, qo, kv, earlier):
    rows = qo[0].shape[1]
    kv_total = heads * members
    group = qo[0].shape[2] // kv_total
    head_dim = kv[0].shape[2] // kv_total
    width = group + 2 * head_dim

    def column(i, me_ref):
        member = i if first is None else me_ref[0] ^ ((first + i) % members)
        return member * heads + head

    qo_spec = pl.BlockSpec((1, rows, group), lambda i, m: (0, 0, column(i, m)))
    kv_spec = pl.BlockSpec((2, rows, head_dim), lambda i, m: (0, 0, column(i, m)))
    earlier = [] if earlier is None else list(earlier)
    ins = [x for pair in zip(qo, kv) for x in pair]
    if first is None:
        slabs = [pltpu.HBM((members, rows, width), BF16)]
        slab_specs = [pl.BlockSpec((1, rows, width), lambda i, m: (i, 0, 0))]
    else:
        slabs = [pltpu.HBM((rows, width), BF16)] * count
        slab_specs = [pl.BlockSpec((rows, width), lambda i, m: (0, 0))] * count
    results = pl.pallas_call(
        functools.partial(input_proj_kernel, first is None, len(slabs), group, head_dim),
        name="adam_in",
        grid_spec=pltpu.PrefetchScalarGridSpec(
            num_scalar_prefetch=1,
            grid=(count,),
            in_specs=[pl.BlockSpec(squares.shape, lambda i, m: (0, 0, 0))]
            + [qo_spec, kv_spec] * 4
            + [ANY] * len(earlier),
            out_specs=[qo_spec, kv_spec] * 3 + slab_specs,
        ),
        out_shape=[pltpu.HBM(x.shape, F32) for x in ins[:6]] + slabs,
        input_output_aliases={10 + n: n for n in range(len(earlier))},
        compiler_params=pltpu.CompilerParams(vmem_limit_bytes=wide_vmem),
        cost_estimate=small_cost,
    )(me, squares, *ins, *earlier)
    return results[:6], results[6:]


def output_proj_kernel(squares_ref, *refs):
    ins, (*outs, slab) = refs[:4], refs[-4:]
    clip = clip_of(squares_ref)
    fresh = adam_math(ins[0][0], ins[1][0], ins[2][0], ins[3][0], clip)
    for n in range(3):
        outs[n][0] = fresh[n]
    width = slab.shape[2]
    for member in range(slab.shape[0]):
        slab[member] = fresh[0][:, member * width : (member + 1) * width].astype(BF16)


def update_output_proj(members, squares, qo, earlier, deps):
    rows = qo[0].shape[1]
    width = qo[0].shape[2] // members
    untouched = list(earlier) + list(deps)
    spec = pl.BlockSpec((1, rows, width), lambda i: (1, 0, i))
    return pl.pallas_call(
        output_proj_kernel,
        name="adam_out",
        grid=(members,),
        in_specs=[pl.BlockSpec(squares.shape, lambda i: (0, 0, 0))]
        + [spec] * 4
        + [ANY] * len(untouched),
        out_specs=[spec] * 3 + [pl.BlockSpec((1, rows, width), lambda i: (i, 0, 0))],
        out_shape=[pltpu.HBM(x.shape, F32) for x in qo[:3]]
        + [pltpu.HBM((members, rows, width), BF16)],
        input_output_aliases={5 + n: n for n in range(len(earlier))},
        compiler_params=pltpu.CompilerParams(vmem_limit_bytes=wide_vmem),
        cost_estimate=small_cost,
    )(squares, *qo, *untouched)


def project_kernel(count, me_ref, shard_ref, x_ref, *refs):
    slabs, (send_ref, keep_ref, mine, other, *scratch) = refs[:count], refs[count:]
    weight = slabs[0]
    if count > 1:
        weight = scratch[0]
        rows = slabs[0].shape[0]
        for place in range(count):
            start = pl.multiple_of((me_ref[0] ^ place) * rows, rows)
            weight[pl.ds(start, rows), :] = slabs[place][...]
    shards, group_rows, _ = x_ref.shape
    for mask in range(shards):
        into = other if mask % 2 else mine
        start = mask // 2 * group_rows
        into[start : start + group_rows, :] = x_ref[shard_ref[0] ^ mask]
    send_ref[...] = jnp.dot(other[...], weight[...], preferred_element_type=F32).astype(BF16)
    keep_ref[...] = jnp.dot(mine[...], weight[...], preferred_element_type=F32)


def project(me, shard, x, slabs, deps):
    shards, group_rows, depth = x.shape
    rows, width = slabs[0].shape
    half = shards // 2 * group_rows
    if rows % 16 and len(slabs) > 1:
        slabs = [xor_order(jnp.stack(slabs), me[0]).reshape(depth, width)]
    count = len(slabs)
    vmem = pl.BlockSpec(memory_space=pltpu.VMEM)
    smem = pl.BlockSpec(memory_space=pltpu.SMEM)

    def body(me_ref, shard_ref, x_ref, *refs):
        project_kernel(count, me_ref, shard_ref, x_ref, *refs[:count], *refs[count + len(deps) :])

    scratch = [pltpu.VMEM((half, depth), BF16)] * 2
    if count > 1:
        scratch.append(pltpu.VMEM((depth, width), BF16))
    return pl.pallas_call(
        body,
        name="project",
        in_specs=[smem, smem] + [vmem] * (1 + count) + [ANY] * len(deps),
        out_specs=[vmem, vmem],
        scratch_shapes=scratch,
        out_shape=[pltpu.HBM((half, width), BF16), pltpu.HBM((half, width), F32)],
        compiler_params=pltpu.CompilerParams(vmem_limit_bytes=kernel_vmem),
        cost_estimate=small_cost,
    )(me, shard, x, *slabs, *deps)


def core_sum_kernel(zones, keep_ref, arrived_ref, *refs):
    own_ref, sends = refs[-zones], refs[len(refs) - zones + 1 :]
    rows = own_ref.shape[0]
    for zone in range(zones):
        span = pl.ds(zone * rows, rows)
        total = keep_ref[span, :] + arrived_ref[span, :].astype(F32)
        if zone == 0:
            own_ref[...] = total
        else:
            sends[zone - 1][...] = total.astype(BF16)


def core_sum(zones, keep, arrived, deps):
    rows, width = keep.shape[0] // zones, keep.shape[1]
    vmem = pl.BlockSpec(memory_space=pltpu.VMEM)
    return pl.pallas_call(
        functools.partial(core_sum_kernel, zones),
        name="core_sum",
        in_specs=[vmem, vmem] + [ANY] * len(deps),
        out_specs=[vmem] * zones,
        out_shape=[pltpu.HBM((rows, width), F32)]
        + [jax.ShapeDtypeStruct((rows, width), BF16)] * (zones - 1),
        compiler_params=pltpu.CompilerParams(vmem_limit_bytes=kernel_vmem),
        cost_estimate=small_cost,
    )(in_hbm(keep), arrived, *deps)


def attend_kernel(zones, *refs):
    lens_ref, cos_ref, sin_ref, gain_ref, key_ref, value_ref = refs[:6]
    parts = refs[6 : 6 + zones]
    out_ref, new_key_ref, new_value_ref, query, mixed = refs[-5:]
    head_dim = new_key_ref.shape[1]
    groups = query.shape[1]
    total = parts[0][...]
    for part in parts[1:]:
        total = total + part[...].astype(F32)
    cosine, sine = cos_ref[...], sin_ref[...]

    def placed(values, gain):
        mean_square = jnp.mean(values * values, axis=-1, keepdims=True)
        values = values * lax.rsqrt(mean_square + eps_norm) * gain
        return values * cosine + pltpu.roll(values, head_dim // 2, 1) * sine

    for group in range(groups):
        columns = total[:, group * head_dim : (group + 1) * head_dim]
        query[:, group, :] = placed(columns, gain_ref[0:1, :])
    new_key = placed(total[:, groups * head_dim : (groups + 1) * head_dim], gain_ref[1:2, :])
    new_key = new_key.astype(BF16)
    new_value = total[:, (groups + 1) * head_dim :].astype(BF16)
    new_key_ref[...] = new_key
    new_value_ref[...] = new_value
    inv_root = 1.0 / math.sqrt(head_dim)
    rotated = query[...].astype(BF16)
    scores = inv_root * lax.dot_general(
        rotated, key_ref[:, 0], (((2,), (2,)), ((0,), (0,))), preferred_element_type=F32
    )
    own_score = inv_root * jnp.sum(
        rotated.astype(F32) * new_key.astype(F32)[:, None, :], axis=-1, keepdims=True
    )
    slots = lax.broadcasted_iota(jnp.int32, scores.shape, 2)
    visible = slots < lens_ref[...][:, None, :]
    masked = jnp.where(visible, scores, -1e30)
    peak = jnp.maximum(jnp.max(masked, axis=-1, keepdims=True), own_score)
    weights = jnp.where(visible, jnp.exp(masked - peak), 0.0)
    own_weight = jnp.exp(own_score - peak)
    inverse = 1.0 / (jnp.sum(weights, axis=-1, keepdims=True) + own_weight)
    own_part = (own_weight * inverse).astype(BF16).astype(F32)
    mixed[...] = (
        lax.dot_general(
            (weights * inverse).astype(BF16),
            value_ref[:, 0],
            (((2,), (1,)), ((0,), (0,))),
            preferred_element_type=F32,
        )
        + own_part * new_value.astype(F32)[:, None, :]
    )
    for group in range(groups):
        out_ref[:, group * head_dim : (group + 1) * head_dim] = mixed[:, group, :].astype(BF16)


def attend(head, parts, lens, cosine, sine, qk_gain, cache, deps):
    rows, width = parts[0].shape
    slots, head_dim = cache[0].shape[2:]
    groups = width // head_dim - 2
    block = 32
    row_block = lambda columns: pl.BlockSpec((block, columns), lambda i: (i, 0))
    cache_block = pl.BlockSpec((block, 1, slots, head_dim), lambda i: (i, head, 0, 0))
    return pl.pallas_call(
        functools.partial(attend_kernel, len(parts)),
        name="attend",
        grid=(rows // block,),
        in_specs=[row_block(slots), row_block(head_dim), row_block(head_dim)]
        + [pl.BlockSpec((2, head_dim), lambda i: (0, 0)), cache_block, cache_block]
        + [row_block(width)] * len(parts)
        + [ANY] * len(deps),
        out_specs=[
            row_block(groups * head_dim),
            row_block(head_dim),
            row_block(head_dim),
        ],
        out_shape=[
            pltpu.HBM((rows, groups * head_dim), BF16),
            jax.ShapeDtypeStruct((rows, head_dim), BF16),
            jax.ShapeDtypeStruct((rows, head_dim), BF16),
        ],
        scratch_shapes=[pltpu.VMEM((block, groups, head_dim), F32)] * 2,
        compiler_params=pltpu.CompilerParams(vmem_limit_bytes=kernel_vmem),
        cost_estimate=small_cost,
    )(lens, cosine, sine, qk_gain, *cache, in_hbm(parts[0]), *parts[1:], *deps)


def stack_rows_kernel(count, *refs):
    parts, out, sems = refs[:count], refs[-2], refs[-1]
    rows = parts[0].shape[0]
    copies = [
        pltpu.make_async_copy(parts[n], out.at[pl.ds(n * rows, rows)], sems.at[n])
        for n in range(count)
    ]
    for copy in copies:
        copy.start()
    for copy in copies:
        copy.wait()


def stack_rows(parts, deps):
    rows, width = parts[0].shape
    return pl.pallas_call(
        functools.partial(stack_rows_kernel, len(parts)),
        name="stack_rows",
        in_specs=[ANY] * (len(parts) + len(deps)),
        out_specs=ANY,
        out_shape=pltpu.HBM((len(parts) * rows, width), BF16),
        scratch_shapes=[pltpu.SemaphoreType.DMA((len(parts),))],
        compiler_params=pltpu.CompilerParams(vmem_limit_bytes=kernel_vmem // 8),
        cost_estimate=small_cost,
    )(*parts, *deps)


def expand_kernel(members, heads, shard_ref, me_ref, *refs):
    att, refs = refs[: 2 * heads], refs[2 * heads :]
    slab, outs, total = refs[0], refs[1 : 1 + members], refs[-1]
    depth = att[0].shape[1]
    shards, share, _ = outs[0].shape
    zones = shards // 2
    for other in range(2):
        part = None
        for head in range(heads):
            term = lax.dot_general(
                att[2 * head + other][...],
                slab[:, head * depth : (head + 1) * depth],
                (((1,), (1,)), ((), ())),
                preferred_element_type=F32,
            )
            part = term if part is None else part + term
        for zone in range(zones):
            shard = shard_ref[0] ^ (2 * zone + other)
            for member in range(members):
                first = (zone * members + member) * share
                total[member, shard] = part[first : first + share, :]
    for mask in range(members):
        outs[mask][...] = total[me_ref[0] ^ mask].astype(outs[mask].dtype)


def expand(shard, me, att, slab):
    heads, members = len(att) // 2, lax.axis_size("tp")
    shards = lax.axis_size("fsdp")
    width = slab.shape[0]
    share = 2 * att[0].shape[0] // (shards * members)
    dtypes = [F32] + [BF16] * (members - 1)
    vmem = pl.BlockSpec(memory_space=pltpu.VMEM)
    smem = pl.BlockSpec(memory_space=pltpu.SMEM)
    return pl.pallas_call(
        functools.partial(expand_kernel, members, heads),
        name="expand",
        in_specs=[smem, smem] + [vmem] * (2 * heads + 1),
        out_specs=[vmem] * members,
        scratch_shapes=[pltpu.VMEM((members, shards, share, width), F32)],
        out_shape=[jax.ShapeDtypeStruct((shards, share, width), dtype) for dtype in dtypes],
        compiler_params=pltpu.CompilerParams(vmem_limit_bytes=kernel_vmem),
        cost_estimate=small_cost,
    )(shard, me, *[in_hbm(a) for a in att], slab)


def member_sum_kernel(*refs):
    total = refs[0][...]
    for share in refs[1:-1]:
        total = total + share[...].astype(F32)
    refs[-1][...] = total.astype(BF16)


def member_sum(shares):
    return pl.pallas_call(
        member_sum_kernel,
        name="member_sum",
        out_shape=jax.ShapeDtypeStruct(shares[0].shape, BF16),
        compiler_params=pltpu.CompilerParams(vmem_limit_bytes=kernel_vmem),
        cost_estimate=small_cost,
    )(*shares)


def finish_kernel(hidden_ref, pieces_ref, out_ref):
    row_terms = jnp.concatenate([pieces_ref[n] for n in range(pieces_ref.shape[0])], axis=1)
    out_ref[...] = (hidden_ref[...].astype(F32) + row_terms.astype(F32)).astype(BF16)


def finish(hidden, pieces):
    return pl.pallas_call(
        finish_kernel,
        name="finish",
        out_shape=jax.ShapeDtypeStruct(hidden.shape, BF16),
        compiler_params=pltpu.CompilerParams(vmem_limit_bytes=kernel_vmem),
        cost_estimate=small_cost,
    )(hidden, pieces)


def angles(positions, head_dim, slots):
    half_dim = head_dim // 2
    frequency = rope_base ** (-(jnp.arange(half_dim, dtype=F32) * 2.0) / head_dim)
    turned = positions.astype(F32)[:, None] * frequency[None, :]
    cosine, sine = jnp.cos(turned), jnp.sin(turned)
    lens = jnp.broadcast_to(positions[:, None], (positions.shape[0], slots))
    return (
        jnp.concatenate([cosine, cosine], axis=1),
        jnp.concatenate([-sine, sine], axis=1),
        lens,
    )


def local(
    master_qo,
    master_kv,
    moment1_qo,
    moment1_kv,
    moment2_qo,
    moment2_kv,
    grad_qo,
    grad_kv,
    hidden,
    norm_gain,
    qk_gain,
    key_cache,
    cached_value_rows,
    lengths,
):
    shards, members = lax.axis_size("fsdp"), lax.axis_size("tp")
    zones = shards // 2
    shard, member = lax.axis_index("fsdp"), lax.axis_index("tp")
    me = member.astype(jnp.int32).reshape(1)
    shard = shard.astype(jnp.int32).reshape(1)
    heads, slots, head_dim = key_cache.shape[1:]

    def swap_member(x, mask):
        return lax.ppermute(x, "tp", xor_perm(members, mask))

    def swap_zone(x, mask):
        return lax.ppermute(x, "fsdp", xor_perm(shards, 2 * mask))

    def swap_core(x):
        return lax.ppermute(x, "fsdp", xor_perm(shards, 1))

    qo = [in_hbm(x) for x in (master_qo, moment1_qo, moment2_qo, grad_qo)]
    kv = [in_hbm(x) for x in (master_kv, moment1_kv, moment2_kv, grad_kv)]
    cache = [in_hbm(key_cache), in_hbm(cached_value_rows)]

    blocks = norm_blocks(shards, members, hidden, norm_gain)
    x = lax.all_to_all(blocks, ("fsdp", "tp"), 0, 0)
    x = x.reshape(shards, -1, blocks.shape[2])

    spread = local_squares(shards * members, qo[3], kv[3])
    squares = lax.all_to_all(spread, ("fsdp", "tp"), 0, 0)

    fresh, slabs = update_input_proj(0, heads, members, 1, members - 1, me, squares, qo, kv, None)
    slabs = [list(slabs)]
    for head in range(1, heads):
        fresh, slab = update_input_proj(
            head, heads, members, None, members, me, squares, qo, kv, fresh
        )
        slabs.append(slab[0])
    fresh, slab = update_input_proj(0, heads, members, 0, 1, me, squares, qo, kv, fresh)
    slabs[0] = list(slab) + slabs[0]
    fresh_kv = fresh[1::2]
    fresh_qo = fresh[0::2]

    cosine, sine, lens = angles(lengths, head_dim, slots)
    parts, latest = [], [slabs[0][0]]
    for head in range(heads):
        if head == 0:
            weights = slabs[0][:1]
            weights += [swap_member(slabs[0][k], k) for k in range(1, members)]
        else:
            weights = lax.all_to_all(tie(slabs[head], send), "tp", 0, 0)
            weights = [weights.reshape(-1, weights.shape[2])]
        send, keep = project(me, shard, x, weights, latest)
        own, *sends = core_sum(zones, keep, swap_core(send), [])
        arrived = [swap_zone(sends[k - 1], k) for k in range(1, zones)]
        parts.append([own] + arrived)
        if head == 0:
            fresh_qo = update_output_proj(members, squares, qo, fresh_qo, sends)
            latest = [fresh_qo[3]] + arrived
    new_keys, new_values, attended = [], [], []
    latest = parts[-1][1:2]
    for head in range(heads):
        rows_out, new_key, new_value = attend(
            head, parts[head], lens, cosine, sine, qk_gain, cache, latest
        )
        new_keys.append(new_key)
        new_values.append(new_value)
        gathered = [rows_out] + [swap_zone(rows_out, k) for k in range(1, zones)]
        latest = gathered[1:2]
        attended.append(stack_rows(gathered, []))
    attended = [x for rows in attended for x in (rows, swap_core(rows))]
    out_slab = lax.all_to_all(tie(fresh_qo[3], send), "tp", 0, 0)
    out_slab = out_slab.reshape(-1, out_slab.shape[2])

    shares = expand(shard, me, attended, out_slab)
    shares = [shares[0]] + [swap_member(shares[k], k) for k in range(1, members)]
    pieces = lax.all_to_all(member_sum(shares), "fsdp", 0, 0)
    new_hidden = finish(hidden, pieces)
    return (
        fresh_qo[0],
        fresh_kv[0],
        fresh_qo[1],
        fresh_kv[1],
        fresh_qo[2],
        fresh_kv[2],
        new_hidden,
        jnp.stack(new_keys, axis=1),
        jnp.stack(new_values, axis=1),
    )


def solution(mesh):
    state = P(None, ("fsdp", "tp"), None)
    return jax.shard_map(
        local,
        mesh=mesh,
        in_specs=(
            state,
            state,
            state,
            state,
            state,
            state,
            state,
            state,
            P(("fsdp", "tp"), None),
            P(),
            P(),
            P("fsdp", "tp", None, None),
            P("fsdp", "tp", None, None),
            P("fsdp"),
        ),
        out_specs=(
            state,
            state,
            state,
            state,
            state,
            state,
            P(("fsdp", "tp"), None),
            P("fsdp", "tp", None),
            P("fsdp", "tp", None),
        ),
        check_vma=False,
    )
```
